256 devices in a mesh: grp: 16 (over z_hi, y), shard: 16 (over x, z_lo, core).
Axes of the slice: x: 4, y: 4, z: 8 (z_hi: 4, z_lo: 2; z = z_hi * 2 + z_lo), core: 2. Of those that a mesh axis runs over, the one named last changes fastest.
Arguments:
- tokens: bfloat16 [32768, 8192], P(('grp', 'shard')), may hold values from -6 to 6
- cotangent: bfloat16 [32768, 16384], P(('grp', 'shard')), may hold values from -6 to 6
- pattern: int32 [96, 2], replicated, may hold values from 0 to 127, as said below
- block_owner: int32 [96], replicated, may hold values from 0 to 15, as said below
- weights: bfloat16 [192, 128, 128], P('shard'), may hold values from -5 to 5
- master: float32 [192, 128, 128], P('shard', 'grp'), may hold values from -5 to 5
- moment_one: float32 [192, 128, 128], P('shard', 'grp'), may hold values from -5 to 5
- moment_two: float32 [192, 128, 128], P('shard', 'grp'), may hold values from 0.5 to 4
Outputs:
- grad_tokens: bfloat16 [32768, 8192], P(('grp', 'shard'))
- new_master: float32 [192, 128, 128], P('shard', 'grp')
- new_moment_one: float32 [192, 128, 128], P('shard', 'grp')
- new_moment_two: float32 [192, 128, 128], P('shard', 'grp')
- new_weights: bfloat16 [192, 128, 128], P('shard')
The draws below stay inside these ranges and needn't reach their ends.
Inputs may be any that keep to these rules, and one draw needn't show every extreme that they name: `pattern`: no two blocks share both their row block and their column block; the row block is below 64 and the column block below 128. `block_owner`: one owner holds at most 12 blocks; in every draw a quarter of the owners hold exactly 12, and every owner holds at least 3.
All inputs are finite; a program needn't handle non-finite values.
Results may differ from the reference program's by a relative error of at most 0.006.
Values may be sent and summed in bfloat16 or wider, within the bound.
A program may use at most 128 MiB of HBM per device.

```python
import math
import jax
import jax.numpy as jnp
from jax import lax

D = 8192
H = 16384
BS = 128
TOK_DEV = 128
BLK_DEV = 6
STEP = 10
CAP = 12
BLOCKS = 96
TOKENS = 32768
N_GRP = 16
N_SHARD = 16


def draw_pattern(key, part):
    key = jax.random.fold_in(key, 11)
    col_blocks = H // BS
    cells = jax.random.permutation(key, D // BS * col_blocks)[:BLOCKS].astype(jnp.int32)
    return jnp.stack([cells // col_blocks, cells % col_blocks], axis=1).astype(jnp.int32)


def draw_block_owner(key, part):
    key = jax.random.fold_in(key, 23)
    key_shift, key_label, key_order = jax.random.split(key, 3)
    quarter = BLK_DEV // 2
    span = 4 * BLK_DEV
    position = jnp.arange(BLOCKS, dtype=jnp.int32)
    quad = position // span
    inside = position % span
    shifts = jax.random.randint(key_shift, (BLOCKS // span,), 0, quarter).astype(jnp.int32)
    shift_here = shifts[quad]
    local_owner = (inside >= CAP).astype(jnp.int32) + (inside >= CAP + quarter + shift_here).astype(jnp.int32) + (inside >= CAP + 3 * quarter).astype(jnp.int32)
    labels = jax.random.permutation(key_label, N_SHARD).astype(jnp.int32)[quad * 4 + local_owner]
    order = jax.random.permutation(key_order, BLOCKS).astype(jnp.int32)
    return labels[order].astype(jnp.int32)


def level_of(key, dims, cuts, smallest, top_value):
    def one(dim, parts):
        heights = jax.random.uniform(jax.random.fold_in(jax.random.fold_in(key, 6), dim), (parts,), jnp.float32, smallest / len(cuts), top_value / len(cuts))
        return jnp.repeat(jnp.exp(heights), dims[dim] // parts).reshape((-1,) + (1,) * (len(dims) - dim - 1))

    gain = one(*cuts[0])
    for cut in cuts[1:]:
        gain = gain * one(*cut)
    return gain


def centred(own_key, extent, scale, bound, pieces=(), held_as=jnp.bfloat16):
    values = scale * jax.random.normal(own_key, extent, jnp.float32)
    if pieces:
        values = values * level_of(own_key, extent, pieces, -0.22, 0.18)
    return jnp.clip(values, -bound, bound).astype(held_as)


def setup_inputs(seed: int = 0) -> dict:
    seeds = jax.random.split(jax.random.key(seed), 9)
    tokens = centred(seeds[0], (TOKENS, D), 1.0, 6.0, ((0, 256),))
    cotangent = centred(seeds[1], (TOKENS, H), 1.0, 6.0, ((0, 256),))
    pattern = draw_pattern(jax.random.fold_in(seeds[8], 71), 0)
    block_owner = draw_block_owner(jax.random.fold_in(seeds[8], 71), 0)
    weights = centred(seeds[4], (N_SHARD * CAP, BS, BS), 1.0, 5.0, ((0, 16),))
    master = centred(seeds[5], (N_SHARD * CAP, BS, BS), 1.0, 5.0, ((0, 16), (1, 16)), jnp.float32)
    moment_one = centred(seeds[6], (N_SHARD * CAP, BS, BS), 1.0, 5.0, ((0, 16), (1, 16)), jnp.float32)
    moment_two = jnp.clip(jnp.exp(math.log(4.0) - 2.0794415 * jax.random.uniform(seeds[7], (N_SHARD * CAP, BS, BS), jnp.float32) ** level_of(seeds[7], (N_SHARD * CAP, BS, BS), ((0, 16), (1, 16)), -0.2, 0.2)), 0.5, 4.0)
    return {"tokens": tokens, "cotangent": cotangent, "pattern": pattern, "block_owner": block_owner, "weights": weights, "master": master, "moment_one": moment_one, "moment_two": moment_two}


def slot_tables(pattern, block_owner, owner_count, capacity):
    onehot = (block_owner[:, None] == jnp.arange(owner_count, dtype=jnp.int32)[None, :]).astype(jnp.int32)
    before = jnp.cumsum(onehot, axis=0) - onehot
    ranking = lax.optimization_barrier(jnp.sum(before * onehot, axis=1)).astype(jnp.int32)
    return (block_owner * capacity + ranking).astype(jnp.int32)

def adam_update(gradient, master, moment_one, moment_two):
    new_one = 0.8 * moment_one + 0.2 * gradient
    new_two = 0.95 * moment_two + 0.05 * gradient * gradient
    first_hat = new_one / (1.0 - 0.8 ** STEP)
    second_hat = new_two / (1.0 - 0.95 ** STEP)
    new_master = master - 0.1 * first_hat / (jnp.sqrt(second_hat) + 1e-08)
    return (new_master, new_one, new_two)

def reference(tokens, cotangent, pattern, block_owner, weights, master, moment_one, moment_two):
    slot_index = slot_tables(pattern, block_owner, N_SHARD, CAP)
    devices = N_GRP * N_SHARD
    weight_scale = 0.5 / math.sqrt(BS)
    grad_scale = 1.0 / math.sqrt(TOKENS)

    def one_block(block_id):
        row_start = (pattern[block_id, 0] * BS).astype(jnp.int32)
        col_start = (pattern[block_id, 1] * BS).astype(jnp.int32)
        rows_part = lax.dynamic_slice_in_dim(tokens, row_start, BS, 1).astype(jnp.float32).reshape(devices, TOK_DEV, BS)
        cols_part = lax.dynamic_slice_in_dim(cotangent, col_start, BS, 1).astype(jnp.float32).reshape(devices, TOK_DEV, BS)
        partial_value = jnp.einsum('ntr,ntc->nrc', rows_part, cols_part)
        rounded = lax.optimization_barrier(partial_value.astype(jnp.bfloat16)).astype(jnp.float32)
        return lax.optimization_barrier(jnp.sum(rounded, axis=0))
    block_grads = lax.map(one_block, jnp.arange(BLOCKS, dtype=jnp.int32))
    gradient = jnp.zeros((N_SHARD * CAP, BS, BS), jnp.float32).at[slot_index].set(block_grads) * grad_scale

    def add_block(running, block_id):
        row_start = (pattern[block_id, 0] * BS).astype(jnp.int32)
        col_start = (pattern[block_id, 1] * BS).astype(jnp.int32)
        block_weight = weights[slot_index[block_id]]
        cols_part = lax.dynamic_slice_in_dim(cotangent, col_start, BS, 1)
        contrib = jnp.dot(cols_part, block_weight.T, preferred_element_type=jnp.float32)
        current = lax.dynamic_slice_in_dim(running, row_start, BS, 1)
        running = lax.dynamic_update_slice_in_dim(running, current + contrib, row_start, 1)
        return (running, None)
    running, unused = lax.scan(add_block, jnp.zeros((TOKENS, D), jnp.float32), jnp.arange(BLOCKS, dtype=jnp.int32))
    grad_tokens = (running * weight_scale).astype(jnp.bfloat16)
    new_master, new_one, new_two = adam_update(gradient, master, moment_one, moment_two)
    return (grad_tokens, new_master, new_one, new_two, new_master.astype(jnp.bfloat16))
```

```python
import functools
import math

import jax
import jax.numpy as jnp
from jax import lax
from jax.experimental import pallas as pl
from jax.experimental.pallas import tpu as pltpu
from jax.sharding import PartitionSpec as P

STEP = 10
BF16 = jnp.bfloat16
F32 = jnp.float32
SIDE = 128
BLOCKS = 96
SLOTS = 192
ROW_BLOCKS = 64
T_PLAIN, T_SORTED, T_SLOT, T_LAST = 0, BLOCKS, 2 * BLOCKS, 2 * BLOCKS + SLOTS


def index_table(pattern, block_owner):
    key = pattern[:, 0] * 128 + pattern[:, 1]
    ids = jnp.arange(BLOCKS, dtype=jnp.int32)
    place = jnp.sum((key[None, :] < key[:, None]).astype(jnp.int32), axis=1)
    earlier = (block_owner[None, :] == block_owner[:, None]) & (ids[None, :] < ids[:, None])
    slot = block_owner * 12 + jnp.sum(earlier.astype(jnp.int32), axis=1)
    twin = (pattern[None, :, 0] == pattern[:, None, 0]) & (key[None, :] < key[:, None])
    packed = (jnp.any(twin, axis=1).astype(jnp.int32) * 16384 + key) * 256 + slot
    in_order = jnp.sum(jnp.where(place[None, :] == ids[:, None], packed[None, :], 0), axis=1)
    slots = jnp.arange(SLOTS, dtype=jnp.int32)
    held = jnp.sum(jnp.where(slot[None, :] == slots[:, None], ids[None, :] + 128, 0), axis=1)
    rows = jnp.arange(ROW_BLOCKS, dtype=jnp.int32)
    here = pattern[None, :, 0] == rows[:, None]
    last = jnp.max(jnp.where(here, place[None, :] + 128, 0), axis=1)
    return jnp.concatenate([key, in_order, held, last])


def field(value, low, bits):
    return lax.shift_right_logical(value, low) & ((1 << bits) - 1)


def choose(bit, zero, one):
    weight = bit.astype(F32)
    return zero * (1.0 - weight) + one * weight


def kernel(
    tbl, tok_h, cot_h, w_h, ma_h, m1_h, m2_h,
    gt_o, nm_o, n1_o, n2_o, nw_o,
    tok, cot, w, ma, m1, m2, nm, n1, n2, nw,
    gp, gr, gb, f1, hb, s1, ib, zr, ga, w1, wall, nwg, res, gout,
    load_sem, out_sem,
    w1_s, w1_r, gc_s, gc_r, gf_s, gf_r, gs_s, gs_r, gz_s, gz_r, ga_s, ga_r,
    wz_s, wz_r, ws_s, ws_r, wf_s, wf_r, wc_s, wc_r, nz_s, nz_r, ny_s, ny_r,
):
    g = lax.axis_index("grp")
    s = lax.axis_index("shard")
    zh, y = g // 4, g % 4
    x, zl, c = s // 4, (s // 2) % 2, s % 2
    z = zh * 2 + zl
    rank = c * 8 + x * 2 + zl
    fa = (1 - c) * x + c * y
    sa = (1 - c) * y + c * x

    def dev(x_, y_, z_, c_):
        return ((z_ // 2) * 4 + y_, x_ * 4 + (z_ % 2) * 2 + c_)

    def dev_f(v):
        return dev((1 - c) * v + c * x, (1 - c) * y + c * v, z, c)

    def dev_s(v):
        return dev((1 - c) * x + c * v, (1 - c) * v + c * y, z, c)

    core = dev(x, y, z, 1 - c)
    pending = []

    def send(src, dst, ss, rs, to):
        cp = pltpu.make_async_remote_copy(
            src_ref=src, dst_ref=dst, send_sem=ss, recv_sem=rs,
            device_id=to, device_id_type=pl.DeviceIdType.MESH,
        )
        cp.start()
        pending.append(cp)

    def arrived(dst, ss, rs):
        pltpu.make_async_remote_copy(
            src_ref=dst, dst_ref=dst, send_sem=ss, recv_sem=rs,
            device_id=core, device_id_type=pl.DeviceIdType.MESH,
        ).wait_recv()

    bar = pltpu.get_barrier_semaphore()
    peers = [(g, (s + d) % 16) for d in range(1, 16)]
    for dz in range(1, 4):
        for l in range(2):
            peers.append((((zh + dz) % 4) * 4 + y, x * 4 + l * 2 + c))
    peers.append((zh * 4 + (y + 1) % 4, s))
    peers.append((zh * 4 + (y + 3) % 4, s))
    for to in peers:
        pl.semaphore_signal(bar, inc=1, device_id=to, device_id_type=pl.DeviceIdType.MESH)

    loads = [
        pltpu.make_async_copy(a, b, load_sem.at[i])
        for i, (a, b) in enumerate(
            [(w_h, w), (tok_h, tok), (cot_h, cot), (ma_h, ma), (m1_h, m1), (m2_h, m2)]
        )
    ]
    for cp in loads:
        cp.start()

    loads[0].wait()
    own = w[:, pl.ds(pl.multiple_of(16 * (g // 2), 16), 16), :].astype(F32)
    half = jnp.where(g % 2 == 0, own[:, :8, :], own[:, 8:, :])
    w1[pl.ds(s * 6, 6)] = half.reshape(6, 16, SIDE).astype(BF16)
    pl.semaphore_wait(bar, len(peers))
    for d in range(1, 16):
        part = w1.at[pl.ds(s * 6, 6)]
        send(part, part, w1_s.at[d], w1_r.at[s], (g, (s + d) % 16))

    loads[1].wait()
    loads[2].wait()

    def partials(h, out, x_):
        sx, sy = 4 - 3 * h, 1 + 3 * h

        def pair(p, carry):
            b0 = h * 48 + x_ * 12 + 2 * p
            prods = []
            for i in range(2):
                key = tbl[T_PLAIN + b0 + i]
                r = field(key, 7, 7) * SIDE
                k = field(key, 0, 7) * SIDE
                prods.append(
                    lax.dot_general(
                        tok[:, pl.ds(r, SIDE)], cot[:, pl.ds(k, SIDE)],
                        (((0,), (0,)), ((), ())), preferred_element_type=F32,
                    )
                )
            for q in range(16):
                lo, hi = 8 * q, 8 * q + 8
                tile = jnp.concatenate([prods[0][lo:hi], prods[1][lo:hi]], axis=0)
                out[x_ * sx + (q % 4) * sy, (q // 4) * 2 + p // 3, p % 3] = tile.astype(BF16)
            return carry

        lax.fori_loop(0, 6, pair, 0)

    for x_ in range(4):
        partials(1 - c, gp, x_)
        for y_ in range(4):
            at = x_ * (4 - 3 * (1 - c)) + y_ * (1 + 3 * (1 - c))
            send(gp.at[at], gr.at[at], gc_s.at[at], gc_r.at[at], core)
    for x_ in range(4):
        partials(c, gb, x_)

    for d in range(1, 16):
        src = (s + d) % 16
        arrived(w1.at[pl.ds(src * 6, 6)], w1_s.at[d], w1_r.at[src])
    mine = fa * 4 + sa
    for p in range(3):
        halves = []
        for i in range(2):
            entry = tbl[T_SORTED + rank * 6 + 2 * p + i]
            tile = w1[field(entry, 1, 7)].astype(F32)
            halves.append(choose(field(entry, 0, 1), tile[:8], tile[8:]))
        wall[c, mine, z, p] = jnp.concatenate(halves, axis=0).astype(BF16)
    for d in range(1, 8):
        to = (z + d) % 8
        part = wall.at[c, mine, z]
        send(part, part, wz_s.at[d], wz_r.at[z], dev(x, y, to, c))

    fp, fm, fo = (fa + 1) % 4, (fa + 3) % 4, (fa + 2) % 4

    def add(dst, *srcs):
        total = dst[...].astype(F32)
        for r in srcs:
            total = total + r[...].astype(F32)
        dst[...] = total.astype(BF16)

    def core_sum(f, lo):
        def one(k, carry):
            at = f * 4 + lo + k
            arrived(gr.at[at], gc_s.at[at], gc_r.at[at])
            add(gb.at[at], gr.at[at])
            return carry

        lax.fori_loop(0, 2, one, 0)

    def loop_add(n, dst, *srcs):
        def one(k, carry):
            add(dst.at[k], *[r.at[k] for r in srcs])
            return carry

        lax.fori_loop(0, n, one, 0)

    core_sum(fo, 0)
    send(gb.at[pl.ds(fo * 4, 2)], f1.at[0], gf_s.at[0], gf_r.at[0], dev_f(fp))
    core_sum(fo, 2)
    send(gb.at[pl.ds(fo * 4 + 2, 2)], f1.at[1], gf_s.at[1], gf_r.at[1], dev_f(fm))
    core_sum(fp, 2)
    send(gb.at[pl.ds(fp * 4 + 2, 2)], f1.at[3], gf_s.at[3], gf_r.at[3], dev_f(fp))
    core_sum(fm, 0)
    send(gb.at[pl.ds(fm * 4, 2)], f1.at[4], gf_s.at[4], gf_r.at[4], dev_f(fm))
    core_sum(fp, 0)
    core_sum(fm, 2)
    core_sum(fa, 0)
    core_sum(fa, 2)

    sp, sm, so = (sa + 1) % 4, (sa + 3) % 4, (sa + 2) % 4
    for d in range(1, 8):
        src = (z + d) % 8
        arrived(wall.at[c, mine, src], wz_s.at[d], wz_r.at[src])
    part = wall.at[c, mine]
    send(part, part, ws_s.at[0], ws_r.at[0], dev_s(sp))
    send(part, part, ws_s.at[1], ws_r.at[1], dev_s(sm))

    arrived(f1.at[0], gf_s.at[0], gf_r.at[0])
    loop_add(2, gb.at[pl.ds(fp * 4, 2)], f1.at[0])
    send(gb.at[pl.ds(fp * 4, 2)], f1.at[2], gf_s.at[2], gf_r.at[2], dev_f(fp))
    arrived(f1.at[1], gf_s.at[1], gf_r.at[1])
    loop_add(2, gb.at[pl.ds(fm * 4 + 2, 2)], f1.at[1])
    send(gb.at[pl.ds(fm * 4 + 2, 2)], f1.at[5], gf_s.at[5], gf_r.at[5], dev_f(fm))

    arrived(wall.at[c, fa * 4 + sm], ws_s.at[0], ws_r.at[0])
    part = wall.at[c, fa * 4 + sm, pl.ds(0, 4)]
    send(part, part, ws_s.at[2], ws_r.at[2], dev_s(sp))
    arrived(wall.at[c, fa * 4 + sp], ws_s.at[1], ws_r.at[1])
    part = wall.at[c, fa * 4 + sp, pl.ds(4, 4)]
    send(part, part, ws_s.at[3], ws_r.at[3], dev_s(sm))

    for k in range(2, 6):
        arrived(f1.at[k], gf_s.at[k], gf_r.at[k])

    def first_total(k, carry):
        total = gb[fa * 4 + k].astype(F32)
        total = total + f1[2 + k // 2, k % 2].astype(F32) + f1[4 + k // 2, k % 2].astype(F32)
        hb[k] = total.astype(BF16)
        return carry

    lax.fori_loop(0, 4, first_total, 0)
    send(hb.at[so, pl.ds(0, 4)], s1.at[0], gs_s.at[0], gs_r.at[0], dev_s(sp))
    send(hb.at[so, pl.ds(4, 4)], s1.at[1], gs_s.at[1], gs_r.at[1], dev_s(sm))
    send(hb.at[sp, pl.ds(4, 4)], s1.at[3], gs_s.at[3], gs_r.at[3], dev_s(sp))
    send(hb.at[sm, pl.ds(0, 4)], s1.at[4], gs_s.at[4], gs_r.at[4], dev_s(sm))

    arrived(wall.at[c, fa * 4 + so, pl.ds(0, 4)], ws_s.at[2], ws_r.at[2])
    arrived(wall.at[c, fa * 4 + so, pl.ds(4, 4)], ws_s.at[3], ws_r.at[3])
    part = wall.at[c, pl.ds(fa * 4, 4)]
    send(part, part, wf_s.at[0], wf_r.at[0], dev_f(fp))
    send(part, part, wf_s.at[1], wf_r.at[1], dev_f(fm))
    send(part, part, wc_s.at[0], wc_r.at[0], core)

    arrived(s1.at[0], gs_s.at[0], gs_r.at[0])
    add(hb.at[sp, pl.ds(0, 4)], s1.at[0])
    send(hb.at[sp, pl.ds(0, 4)], s1.at[2], gs_s.at[2], gs_r.at[2], dev_s(sp))
    arrived(s1.at[1], gs_s.at[1], gs_r.at[1])
    add(hb.at[sm, pl.ds(4, 4)], s1.at[1])
    send(hb.at[sm, pl.ds(4, 4)], s1.at[5], gs_s.at[5], gs_r.at[5], dev_s(sm))
    for k in range(2, 6):
        arrived(s1.at[k], gs_s.at[k], gs_r.at[k])
    for k in range(2):
        part = pl.ds(4 * k, 4)
        total = hb[sa, part].astype(F32) + s1[2 + k].astype(F32) + s1[4 + k].astype(F32)
        ib[part] = total.astype(BF16)

    for d in range(1, 8):
        to = (z + d) % 8
        send(ib.at[to], zr.at[z], gz_s.at[d], gz_r.at[z], dev(x, y, to, c))

    arrived(wall.at[c, pl.ds(fm * 4, 4)], wf_s.at[0], wf_r.at[0])
    part = wall.at[c, pl.ds(fm * 4, 2)]
    send(part, part, wf_s.at[2], wf_r.at[2], dev_f(fp))
    arrived(wall.at[c, pl.ds(fp * 4, 4)], wf_s.at[1], wf_r.at[1])
    part = wall.at[c, pl.ds(fp * 4 + 2, 2)]
    send(part, part, wf_s.at[3], wf_r.at[3], dev_f(fm))
    part = wall.at[c, pl.ds(fm * 4, 4)]
    send(part, part, wc_s.at[1], wc_r.at[1], core)
    part = wall.at[c, pl.ds(fp * 4, 4)]
    send(part, part, wc_s.at[2], wc_r.at[2], core)

    total = ib[z].astype(F32)
    for d in range(1, 8):
        src = (z + d) % 8
        arrived(zr.at[src], gz_s.at[d], gz_r.at[src])
        total = total + zr[src].astype(F32)
    ga[pl.ds(rank * 3, 3)] = total.astype(BF16)
    for d in range(1, 16):
        part = ga.at[pl.ds(rank * 3, 3)]
        send(part, part, ga_s.at[d], ga_r.at[s], (g, (s + d) % 16))

    arrived(wall.at[c, pl.ds(fo * 4, 2)], wf_s.at[2], wf_r.at[2])
    arrived(wall.at[c, pl.ds(fo * 4 + 2, 2)], wf_s.at[3], wf_r.at[3])
    part = wall.at[c, pl.ds(fo * 4, 4)]
    send(part, part, wc_s.at[3], wc_r.at[3], core)

    for k in range(3, 6):
        loads[k].wait()
    for d in range(1, 16):
        src = (s + d) % 16
        at = (src % 2) * 8 + (src // 4) * 2 + (src // 2) % 2
        arrived(ga.at[pl.ds(at * 3, 3)], ga_s.at[d], ga_r.at[src])
    scale = 1.0 / math.sqrt(256 * SIDE)
    for k in range(12):
        held = tbl[T_SLOT + s * 12 + k]
        tile = ga[field(held, 1, 6)].astype(F32)
        grad = choose(field(held, 0, 1), tile[:8], tile[8:])
        grad = grad * (field(held, 7, 1).astype(F32) * scale)
        one = 0.8 * m1[k] + 0.2 * grad
        two = 0.95 * m2[k] + 0.05 * grad * grad
        n1[k] = one
        n2[k] = two
        nm[k] = ma[k] - 0.1 * (one / (1.0 - 0.8**STEP)) / (
            jnp.sqrt(two / (1.0 - 0.95**STEP)) + 1e-08
        )
    for p in range(6):
        nwg[y, zh, p] = nm[2 * p : 2 * p + 2].reshape(16, SIDE).astype(BF16)
    for d in range(1, 4):
        part = nwg.at[y, zh]
        send(part, part, nz_s.at[d], nz_r.at[zh], dev(x, y, ((zh + d) % 4) * 2 + zl, c))
    outs = [
        pltpu.make_async_copy(a, b, out_sem.at[i])
        for i, (a, b) in enumerate([(nm, nm_o), (n1, n1_o), (n2, n2_o)])
    ]
    for cp in outs:
        cp.start()

    yp, ym, yo = (y + 1) % 4, (y + 3) % 4, (y + 2) % 4

    def contributions(h, acc0):
        sx, sy = 4 - 3 * h, 1 + 3 * h

        def pair(pj, acc):
            x_, zl_, p = pj // 6, (pj // 3) % 2, pj % 3
            lows, highs = [], []
            for q in range(16):
                tile = wall[h, x_ * sx + (q % 4) * sy, (q // 4) * 2 + zl_, p].astype(F32)
                lows.append(tile[:8])
                highs.append(tile[8:])
            for i, rows in enumerate((lows, highs)):
                j = h * 48 + 2 * pj + i
                entry = tbl[T_SORTED + j]
                k = field(entry, 8, 7) * SIDE
                block = jnp.concatenate(rows, axis=0).astype(BF16)
                part = lax.dot_general(
                    cot[:, pl.ds(k, SIDE)], block,
                    (((1,), (1,)), ((), ())), preferred_element_type=F32,
                )
                acc = acc * field(entry, 22, 1).astype(F32) + part
                res[j] = (acc * (0.5 / math.sqrt(SIDE))).astype(BF16)
            return acc

        return lax.fori_loop(0, 24, pair, acc0)

    for d in range(1, 4):
        src = (zh + d) % 4
        arrived(nwg.at[y, src], nz_s.at[d], nz_r.at[src])
    send(nwg.at[y], nwg.at[y], ny_s.at[0], ny_r.at[0], dev(x, yp, z, c))
    send(nwg.at[y], nwg.at[y], ny_s.at[1], ny_r.at[1], dev(x, ym, z, c))

    oa = (1 - c) * y + c * x
    for k, v in enumerate((oa, (oa + 3) % 4, (oa + 1) % 4, (oa + 2) % 4)):
        arrived(wall.at[1 - c, pl.ds(v * 4, 4)], wc_s.at[k], wc_r.at[k])
    acc = contributions(0, jnp.zeros((SIDE, SIDE), F32))

    arrived(nwg.at[ym], ny_s.at[0], ny_r.at[0])
    part = nwg.at[ym, pl.ds(0, 2)]
    send(part, part, ny_s.at[2], ny_r.at[2], dev(x, yp, z, c))
    arrived(nwg.at[yp], ny_s.at[1], ny_r.at[1])
    part = nwg.at[yp, pl.ds(2, 2)]
    send(part, part, ny_s.at[3], ny_r.at[3], dev(x, ym, z, c))

    contributions(1, acc)

    for quarter in range(4):
        def place(r, carry):
            last = tbl[T_LAST + r]
            value = res[field(last, 0, 7)].astype(F32) * field(last, 7, 1).astype(F32)
            gout[:, pl.ds(pl.multiple_of(r * SIDE, SIDE), SIDE)] = value.astype(BF16)
            return carry

        lax.fori_loop(16 * quarter, 16 * quarter + 16, place, 0)
        part = pl.ds(quarter * 16 * SIDE, 16 * SIDE)
        cp = pltpu.make_async_copy(gout.at[:, part], gt_o.at[:, part], out_sem.at[3 + quarter])
        cp.start()
        outs.append(cp)

    arrived(nwg.at[yo, pl.ds(0, 2)], ny_s.at[2], ny_r.at[2])
    arrived(nwg.at[yo, pl.ds(2, 2)], ny_s.at[3], ny_r.at[3])

    def unfold(p, carry):
        for q in range(8):
            a = nwg[(2 * q) % 4, (2 * q) // 4, p].astype(F32)
            b = nwg[(2 * q + 1) % 4, (2 * q + 1) // 4, p].astype(F32)
            nw[2 * p, pl.ds(16 * q, 16)] = jnp.concatenate([a[:8], b[:8]], axis=0).astype(BF16)
            nw[2 * p + 1, pl.ds(16 * q, 16)] = jnp.concatenate([a[8:], b[8:]], axis=0).astype(BF16)
        return carry

    lax.fori_loop(0, 6, unfold, 0)
    cp = pltpu.make_async_copy(nw, nw_o, out_sem.at[7])
    cp.start()
    outs.append(cp)
    for cp in outs:
        cp.wait()
    for cp in pending:
        cp.wait_send()


def body(tokens, cotangent, pattern, block_owner, weights, master, moment_one, moment_two):
    table = index_table(pattern, block_owner)
    any_spec = pl.BlockSpec(memory_space=pl.ANY)
    rows = (12, 8, SIDE)
    v = pltpu.VMEM
    dma = pltpu.SemaphoreType.DMA
    tile = (3, 16, SIDE)
    sems = [16, 16, 16, 16, 6, 6, 6, 6, 8, 8, 16, 16, 8, 8, 4, 4, 4, 4, 4, 4, 4, 4, 4, 4]
    scratch = [
        v(tokens.shape, BF16), v(cotangent.shape, BF16), v(weights.shape, BF16),
        v(rows, F32), v(rows, F32), v(rows, F32),
        v(rows, F32), v(rows, F32), v(rows, F32), v((12, SIDE, SIDE), BF16),
        v((16, 8) + tile, BF16), v((16, 8) + tile, BF16), v((16, 8) + tile, BF16),
        v((6, 2, 8) + tile, BF16),
        v((4, 8) + tile, BF16), v((6, 4) + tile, BF16),
        v((8,) + tile, BF16), v((8,) + tile, BF16),
        v((48, 16, SIDE), BF16), v((96, 16, SIDE), BF16),
        v((2, 16, 8) + tile, BF16),
        v((4, 4, 6, 16, SIDE), BF16),
        v((BLOCKS, SIDE, SIDE), BF16), v(tokens.shape, BF16),
        dma((6,)), dma((8,)),
    ] + [dma((n,)) for n in sems]
    return pl.pallas_call(
        kernel,
        out_shape=(
            jax.ShapeDtypeStruct(tokens.shape, BF16),
            jax.ShapeDtypeStruct(rows, F32),
            jax.ShapeDtypeStruct(rows, F32),
            jax.ShapeDtypeStruct(rows, F32),
            jax.ShapeDtypeStruct(weights.shape, BF16),
        ),
        in_specs=[pl.BlockSpec(memory_space=pltpu.SMEM)] + [any_spec] * 6,
        out_specs=(any_spec,) * 5,
        scratch_shapes=scratch,
        compiler_params=pltpu.CompilerParams(
            collective_id=0, has_side_effects=True, vmem_limit_bytes=48 * 1024 * 1024
        ),
    )(table, tokens, cotangent, weights, master, moment_one, moment_two)


def solution(mesh):
    return jax.shard_map(
        body,
        mesh=mesh,
        in_specs=(
            P(("grp", "shard"), None),
            P(("grp", "shard"), None),
            P(),
            P(),
            P("shard", None, None),
            P("shard", "grp", None),
            P("shard", "grp", None),
            P("shard", "grp", None),
        ),
        out_specs=(
            P(("grp", "shard"), None),
            P("shard", "grp", None),
            P("shard", "grp", None),
            P("shard", "grp", None),
            P("shard", None, None),
        ),
        check_vma=False,
    )
```
